32 devices in a mesh: dp: 8 (over z, y), tensor: 4 (over x, core).
Axes of the slice: x: 2, y: 2, z: 4, core: 2. Of those that a mesh axis runs over, the one named last changes fastest.
Arguments:
- context: bfloat16 [4096, 1024], P('dp', 'tensor'), may hold values from -6 to 6
- w_out: bfloat16 [1024, 4096], P('tensor'), may hold values from -0.375 to 0.375
- encoder: bfloat16 [4096, 512], replicated, may hold values from -0.09375 to 0.09375
- decoder: bfloat16 [2048, 4096], P(None, 'tensor'), may hold values from -0.125 to 0.125
- out_grad: bfloat16 [4096, 4096], P('dp', 'tensor'), may hold values from -6 to 6
Outputs:
- mixed: bfloat16 [4096, 4096], P('dp', 'tensor')
- grad_context: bfloat16 [4096, 1024], P('dp', 'tensor')
- grad_wout: float32 [4096, 1024], P('dp', 'tensor')
The draws below stay inside these ranges and needn't reach their ends.
All inputs are finite; a program needn't handle non-finite values.
Results may differ from the reference program's by a relative error of at most 0.0057.
Values may be sent and summed in bfloat16 or wider, within the bound.
A program may use at most 128 MiB of HBM per device.

```python
import jax
import jax.numpy as jnp
from jax import lax

D = 4096
CODE = 512
HEAD_DIM = 128
HEAD_DEV = 2
TOKENS = 4096
HEADS = 8
DEC_IN = 2048
N_DP = 8
N_TENSOR = 4


def block_scale(own_key, dims, cuts, least, top_value):
    level = 1.0
    for position, blocks in cuts:
        heights = jax.random.uniform(jax.random.fold_in(jax.random.fold_in(own_key, 6), position), (blocks,), jnp.float32, least / len(cuts), top_value / len(cuts))
        level = level * jnp.repeat(jnp.exp(heights), dims[position] // blocks).reshape((-1,) + (1,) * (len(dims) - 1 - position))
    return level


def noise(own_key, shape, scale, bound, shards=(), kind=jnp.bfloat16):
    array = scale * jax.random.normal(own_key, shape, jnp.float32)
    if shards:
        array = array * block_scale(own_key, shape, shards, -0.22, 0.18)
    return jnp.clip(array, -bound, bound).astype(kind)


def setup_inputs(seed: int = 0) -> dict:
    splits = jax.random.split(jax.random.key(seed), 6)
    return {
        "context": noise(splits[0], (TOKENS, HEADS * HEAD_DIM), 1.0, 6.0, ((0, 8), (1, 4))),
        "w_out": noise(splits[1], (HEADS * HEAD_DIM, D), (HEAD_DEV * HEAD_DIM) ** -0.5, 0.375, ((0, 4),)),
        "encoder": noise(splits[2], (D, CODE), D ** -0.5, 0.09375),
        "decoder": noise(splits[3], (DEC_IN, D), DEC_IN ** -0.5, 0.125, ((1, 4),)),
        "out_grad": noise(splits[4], (TOKENS, D), 1.0, 6.0, ((0, 8), (1, 4))),
    }


def reference(context, w_out, encoder, decoder, out_grad):
    width = HEAD_DEV * HEAD_DIM
    ctx_parts = context.reshape(TOKENS, N_TENSOR, width).transpose(1, 0, 2)
    wout_parts = w_out.reshape(N_TENSOR, width, D)
    dec_parts = decoder.reshape(N_TENSOR, CODE, D)

    def one_source(total, pieces):
        ctx_piece, wout_piece, dec_piece = pieces
        partial_value = jnp.dot(ctx_piece, wout_piece, preferred_element_type=jnp.float32).astype(jnp.bfloat16)
        code = jnp.dot(partial_value, encoder, preferred_element_type=jnp.float32).astype(jnp.bfloat16)
        total = total + jnp.dot(code, dec_piece, preferred_element_type=jnp.float32)
        code_grad = lax.dot_general(out_grad, dec_piece, (((1,), (1,)), ((), ())), preferred_element_type=jnp.float32).astype(jnp.bfloat16)
        part_grad = lax.dot_general(code_grad, encoder, (((1,), (1,)), ((), ())), preferred_element_type=jnp.float32).astype(jnp.bfloat16)
        ctx_grad = lax.dot_general(part_grad, wout_piece, (((1,), (1,)), ((), ())), preferred_element_type=jnp.float32).astype(jnp.bfloat16)
        wout_grad = lax.dot_general(part_grad, ctx_piece, (((0,), (0,)), ((), ())), preferred_element_type=jnp.float32) / N_DP
        return total, (ctx_grad, wout_grad)

    start = jnp.zeros((TOKENS, D), jnp.float32)
    total, stacked = lax.scan(one_source, start, (ctx_parts, wout_parts, dec_parts))
    ctx_grads, wout_grads = stacked
    mixed = total.astype(jnp.bfloat16)
    grad_context = ctx_grads.transpose(1, 0, 2).reshape(TOKENS, N_TENSOR * width)
    grad_wout = wout_grads.transpose(1, 0, 2).reshape(D, N_TENSOR * width)
    return mixed, grad_context, grad_wout
```

```python
import jax
import jax.numpy as jnp
from jax import lax
from jax.sharding import PartitionSpec as P


def dot(a, b, ca, cb):
    return lax.dot_general(a, b, (((ca,), (cb,)), ((), ())), preferred_element_type=jnp.float32)


def on_device(context, w_out, encoder, decoder, out_grad):
    replicas = lax.axis_size("dp")
    own_rows = encoder.shape[0] // replicas
    product = dot(w_out, encoder, 1, 0).astype(jnp.bfloat16)
    code = dot(context, product, 1, 0).astype(jnp.bfloat16)
    mixed = dot(lax.all_gather(code, "tensor", axis=1, tiled=True), decoder, 1, 0).astype(jnp.bfloat16)
    grad_codes = lax.psum_scatter(
        dot(decoder, out_grad, 1, 1), "tensor", scatter_dimension=0, tiled=True
    ).astype(jnp.bfloat16)
    grad_context = dot(grad_codes, product, 0, 1).astype(jnp.bfloat16)
    inner = lax.psum(dot(grad_codes, context, 1, 0), "dp").astype(jnp.bfloat16)
    rows = lax.dynamic_slice_in_dim(encoder, lax.axis_index("dp") * own_rows, own_rows, 0)
    grad_wout = dot(rows, inner, 1, 0) / replicas
    return (mixed, grad_context, grad_wout)


def solution(mesh):
    in_specs = (P("dp", "tensor"), P("tensor", None), P(), P(None, "tensor"), P("dp", "tensor"))
    out_specs = (P("dp", "tensor"), P("dp", "tensor"), P("dp", "tensor"))
    return jax.shard_map(
        on_device, mesh=mesh, in_specs=in_specs, out_specs=out_specs, check_vma=False
    )
```

```python
import functools

import jax
import jax.numpy as jnp
from jax import lax
from jax.experimental import pallas as pl
from jax.experimental.pallas import tpu as pltpu
from jax.sharding import PartitionSpec as P

BF16, F32 = jnp.bfloat16, jnp.float32
CHUNKS = 2


def dot(a, b, ca, cb):
    return lax.dot_general(a, b, (((ca,), (cb,)), ((), ())), preferred_element_type=F32)


def kernel(
    S, R,
    ctx_h, w_h, enc_h, dec_h, og_h,
    mixed_h, gctx_h, gw_h,
    ctx, w, enc, dec, og,
    we, codes, pair_out, pair_in, chip_out, chip_in, cg_own, cg,
    gt_own, gt_out, gt_in, gt_all, acc, mixed, gctx, gw,
    load_sem, dec_sem, store_sem, mix_sem,
    pair_ss, pair_rs, chip_ss, chip_rs, near_ss, far_ss, fwd_ss, code_rs,
    sum_ss, sum_rs, all_ss, all_rs,
):
    K = S // 2
    T, HW = ctx.shape
    C = we.shape[1]
    D = enc.shape[0]
    part = HW // R
    own_rows = D // R
    step = T // CHUNKS
    d, t = lax.axis_index("dp"), lax.axis_index("tensor")
    k, c = t // 2, lax.rem(t, 2)
    mate = 2 * k + 1 - c

    def chip(o):
        return lax.rem(k + o, K)

    def rows(ch):
        return pl.ds(pl.multiple_of(ch * step, step), step)

    def block(j):
        return pl.ds(pl.multiple_of(j * C, C), C)

    def piece(r):
        return pl.ds(pl.multiple_of(r * part, part), part)

    def remote(src, dst, ss, rs, **where):
        return pltpu.make_async_remote_copy(
            src_ref=src, dst_ref=dst, send_sem=ss, recv_sem=rs,
            device_id=where, device_id_type=pl.DeviceIdType.MESH,
        )

    def load(i, src, dst):
        return pltpu.make_async_copy(src, dst, load_sem.at[i])

    def load_dec(j):
        return pltpu.make_async_copy(dec_h.at[block(j), :], dec.at[block(j), :], dec_sem.at[j])

    load_og = load(0, og_h, og)
    load_w, load_enc, load_ctx = load(1, w_h, w), load(2, enc_h, enc), load(3, ctx_h, ctx)
    load_og.start()

    @pl.loop(0, K)
    def _(i):
        o = lax.rem(i + 1, K)
        load_dec(2 * chip(o) + 1 - c).start()
        load_dec(2 * chip(o) + c).start()

    load_w.start()
    load_enc.start()
    load_ctx.start()

    barrier = pltpu.get_barrier_semaphore()
    MESH = pl.DeviceIdType.MESH
    pl.semaphore_signal(barrier, inc=1, device_id={"tensor": mate}, device_id_type=MESH)

    @pl.loop(1, K)
    def _(o):
        pl.semaphore_signal(barrier, inc=1, device_id={"tensor": 2 * chip(o) + c}, device_id_type=MESH)

    @pl.loop(1, R)
    def _(o):
        pl.semaphore_signal(barrier, inc=1, device_id={"dp": lax.rem(d + o, R)}, device_id_type=MESH)

    pl.semaphore_wait(barrier, 1 + (K - 1) + (R - 1))

    def pair_copy(o, ch):
        return remote(pair_out.at[o, rows(ch), :], pair_in.at[o, rows(ch), :],
                      pair_ss.at[o, ch], pair_rs.at[o, ch], tensor=mate)

    def chip_copy(o, ch):
        return remote(chip_out.at[o, rows(ch), :], chip_in.at[o, rows(ch), :],
                      chip_ss.at[o, ch], chip_rs.at[o, ch], tensor=2 * chip(o) + c)

    load_og.wait()

    def for_mate(o):
        j = 2 * chip(o) + 1 - c
        load_dec(j).wait()

        @pl.loop(0, CHUNKS)
        def _(ch):
            pair_out[o, rows(ch), :] = dot(og[rows(ch), :], dec[block(j), :], 1, 1).astype(BF16)
            pair_copy(o, ch).start()

    @pl.loop(1, K)
    def _(o):
        for_mate(o)
        j = 2 * chip(o) + c
        load_dec(j).wait()

        @pl.loop(0, CHUNKS)
        def _(ch):
            cg_own[rows(ch), :] = dot(og[rows(ch), :], dec[block(j), :], 1, 1)
            pair_copy(o, ch).wait_recv()
            chip_out[o, rows(ch), :] = (
                cg_own[rows(ch), :] + pair_in[o, rows(ch), :].astype(F32)
            ).astype(BF16)
            chip_copy(o, ch).start()

    for_mate(0)
    load_dec(t).wait()

    @pl.loop(0, CHUNKS)
    def _(ch):
        cg_own[rows(ch), :] = dot(og[rows(ch), :], dec[block(t), :], 1, 1)

    load_w.wait()
    load_enc.wait()
    we[...] = dot(w[...], enc[...], 1, 0).astype(BF16)
    load_ctx.wait()

    def near_copy(j):
        return remote(codes.at[j], codes.at[j], near_ss, code_rs.at[j, 0], tensor=mate)

    def far_copy(j, o, ch):
        return remote(codes.at[j, rows(ch), :], codes.at[j, rows(ch), :],
                      far_ss.at[o, ch], code_rs.at[j, ch], tensor=2 * chip(o) + c)

    def fwd_copy(j, o, ch):
        return remote(codes.at[j, rows(ch), :], codes.at[j, rows(ch), :],
                      fwd_ss.at[o, ch], code_rs.at[j, ch], tensor=mate)

    codes[t] = dot(ctx[...], we[...], 1, 0).astype(BF16)
    near_copy(t).start()

    @pl.loop(0, CHUNKS)
    def _(ch):
        acc[rows(ch), :] = dot(codes[t, rows(ch), :], dec[block(t), :], 1, 0)

    near_copy(mate).wait_recv()

    @pl.loop(0, CHUNKS)
    def _(ch):
        acc[rows(ch), :] += dot(codes[mate, rows(ch), :], dec[block(mate), :], 1, 0)

    @pl.loop(1, K)
    def _(o):
        @pl.loop(0, CHUNKS)
        def _(ch):
            chip_copy(o, ch).wait_send()
            far_copy(t, o, ch).start()

    @pl.loop(0, CHUNKS)
    def _(ch):
        pair_copy(0, ch).wait_recv()
        cg_own[rows(ch), :] += pair_in[0, rows(ch), :].astype(F32)

        @pl.loop(1, K)
        def _(o):
            chip_copy(o, ch).wait_recv()
            cg_own[rows(ch), :] += chip_in[o, rows(ch), :].astype(F32)

        cg[rows(ch), :] = cg_own[rows(ch), :].astype(BF16)

    def sum_copy(o):
        return remote(gt_out.at[piece(lax.rem(d + o, R)), :], gt_in.at[o],
                      sum_ss.at[o], sum_rs.at[o], dp=lax.rem(d + o, R))

    def all_copy(r, o):
        return remote(gt_all.at[piece(r), :], gt_all.at[piece(r), :],
                      all_ss.at[o], all_rs.at[o], dp=lax.rem(d + o, R))

    gt_own[...] = dot(ctx[...], cg[...], 0, 0)
    gt_out[...] = gt_own[...].astype(BF16)

    @pl.loop(1, R)
    def _(o):
        sum_copy(o).start()

    gctx[...] = dot(cg[...], we[...], 1, 1).astype(BF16)
    store_gctx = pltpu.make_async_copy(gctx, gctx_h, store_sem.at[0])
    store_gctx.start()

    @pl.loop(1, R)
    def _(o):
        sum_copy(o).wait_recv()
        gt_own[piece(d), :] += gt_in[o].astype(F32)

    gt_all[piece(d), :] = gt_own[piece(d), :].astype(BF16)

    @pl.loop(1, R)
    def _(o):
        all_copy(d, o).start()

    @pl.loop(0, CHUNKS)
    def _(ch):
        @pl.loop(1, K)
        def _(o):
            j = 2 * lax.rem(k - o + K, K) + c
            far_copy(j, o, ch).wait_recv()
            fwd_copy(j, o, ch).start()
            acc[rows(ch), :] += dot(codes[j, rows(ch), :], dec[block(j), :], 1, 0)

    @pl.loop(1, R)
    def _(o):
        all_copy(lax.rem(d - o + R, R), o).wait_recv()

    mine = pl.ds(pl.multiple_of(d * own_rows, own_rows), own_rows)
    gw[...] = dot(enc[mine, :], gt_all[...], 1, 1) * (1.0 / R)
    store_gw = pltpu.make_async_copy(gw, gw_h, store_sem.at[1])
    store_gw.start()

    def store_mixed(ch):
        return pltpu.make_async_copy(mixed.at[rows(ch), :], mixed_h.at[rows(ch), :], mix_sem.at[ch])

    @pl.loop(0, CHUNKS)
    def _(ch):
        @pl.loop(1, K)
        def _(o):
            j = 2 * lax.rem(k - o + K, K) + 1 - c
            fwd_copy(j, o, ch).wait_recv()
            acc[rows(ch), :] += dot(codes[j, rows(ch), :], dec[block(j), :], 1, 0)

        mixed[rows(ch), :] = acc[rows(ch), :].astype(BF16)
        store_mixed(ch).start()

    near_copy(t).wait_send()

    @pl.loop(0, CHUNKS)
    def _(ch):
        pair_copy(0, ch).wait_send()

        @pl.loop(1, K)
        def _(o):
            pair_copy(o, ch).wait_send()
            far_copy(t, o, ch).wait_send()
            fwd_copy(2 * lax.rem(k - o + K, K) + c, o, ch).wait_send()

        store_mixed(ch).wait()

    @pl.loop(1, R)
    def _(o):
        sum_copy(o).wait_send()
        all_copy(d, o).wait_send()

    store_gctx.wait()
    store_gw.wait()


def on_device(S, R, context, w_out, encoder, decoder, out_grad):
    T, HW = context.shape
    D, C = encoder.shape
    DL = out_grad.shape[1]
    K = S // 2
    hbm = pl.BlockSpec(memory_space=pl.ANY)
    dma = pltpu.SemaphoreType.DMA
    shapes = [
        ((T, HW), BF16), ((HW, D), BF16), ((D, C), BF16), ((S * C, DL), BF16), ((T, DL), BF16),
        ((HW, C), BF16), ((S, T, C), BF16),
        ((K, T, C), BF16), ((K, T, C), BF16), ((K, T, C), BF16), ((K, T, C), BF16),
        ((T, C), F32), ((T, C), BF16),
        ((HW, C), F32), ((HW, C), BF16), ((R, HW // R, C), BF16), ((HW, C), BF16),
        ((T, DL), F32), ((T, DL), BF16), ((T, HW), BF16), ((D // R, HW), F32),
    ]
    sems = [
        dma((4,)), dma((S,)), dma((2,)), dma((CHUNKS,)),
        dma((K, CHUNKS)), dma((K, CHUNKS)), dma((K, CHUNKS)), dma((K, CHUNKS)),
        dma, dma((K, CHUNKS)), dma((K, CHUNKS)), dma((S, CHUNKS)),
        dma((R,)), dma((R,)), dma((R,)), dma((R,)),
    ]
    return pl.pallas_call(
        functools.partial(kernel, S, R),
        out_shape=(
            jax.ShapeDtypeStruct((T, DL), BF16),
            jax.ShapeDtypeStruct((T, HW), BF16),
            jax.ShapeDtypeStruct((D // R, HW), F32),
        ),
        in_specs=[hbm] * 5,
        out_specs=(hbm,) * 3,
        scratch_shapes=[pltpu.VMEM(s, dt) for s, dt in shapes] + sems,
        compiler_params=pltpu.CompilerParams(
            collective_id=0, has_side_effects=True, vmem_limit_bytes=56 * 1024 * 1024
        ),
        cost_estimate=pl.CostEstimate(flops=6_000_000_000, bytes_accessed=14_000_000, transcendentals=0),
    )(context, w_out, encoder, decoder, out_grad)


def solution(mesh):
    S, R = mesh.shape["tensor"], mesh.shape["dp"]
    in_specs = (P("dp", "tensor"), P("tensor", None), P(), P(None, "tensor"), P("dp", "tensor"))
    out_specs = (P("dp", "tensor"), P("dp", "tensor"), P("dp", "tensor"))
    return jax.shard_map(
        functools.partial(on_device, S, R), mesh=mesh, in_specs=in_specs, out_specs=out_specs, check_vma=False
    )
```

```python
import functools

import jax
import jax.numpy as jnp
from jax import lax
from jax.experimental import pallas as pl
from jax.experimental.pallas import tpu as pltpu
from jax.sharding import PartitionSpec as P

BF16, F32 = jnp.bfloat16, jnp.float32
CHUNKS = 2
PARTS = 4


def dot(a, b, ca, cb):
    return lax.dot_general(a, b, (((ca,), (cb,)), ((), ())), preferred_element_type=F32)


def kernel(
    S, R,
    ctx_h, w_h, enc_h, dec_h, og_h,
    mixed_h, gctx_h, gw_h,
    ctx, w, enc, dec, og,
    we, codes, pair_out, pair_in, chip_out, chip_in, cg_own, cg,
    gt_own, gt_out, gt_in, gt_all, acc, mixed, gctx, gw,
    load_sem, dec_sem, store_sem, mix_sem,
    pair_ss, pair_rs, chip_ss, chip_rs, near_ss, far_ss, fwd_ss, code_rs,
    sum_ss, sum_rs, all_ss, all_rs,
):
    K = S // 2
    T, HW = ctx.shape
    C = we.shape[1]
    D = enc.shape[0]
    part = HW // R
    own_rows = D // R
    step = T // CHUNKS
    cut = C // CHUNKS
    d, t = lax.axis_index("dp"), lax.axis_index("tensor")
    k, c = t // 2, lax.rem(t, 2)
    mate = 2 * k + 1 - c

    def chip(o):
        return lax.rem(k + o, K)

    def rows(ch):
        return pl.ds(pl.multiple_of(ch * step, step), step)

    def block(j):
        return pl.ds(pl.multiple_of(j * C, C), C)

    def codes_of(j, ch):
        return pl.ds(pl.multiple_of(j * C + ch * cut, cut), cut)

    def piece(r):
        return pl.ds(pl.multiple_of(r * part, part), part)

    def remote(src, dst, ss, rs, **where):
        return pltpu.make_async_remote_copy(
            src_ref=src, dst_ref=dst, send_sem=ss, recv_sem=rs,
            device_id=where, device_id_type=pl.DeviceIdType.MESH,
        )

    def load(i, src, dst):
        return pltpu.make_async_copy(src, dst, load_sem.at[i])

    def load_dec(j):
        return pltpu.make_async_copy(dec_h.at[block(j), :], dec.at[block(j), :], dec_sem.at[j])

    load_og = load(0, og_h, og)
    load_w, load_enc, load_ctx = load(1, w_h, w), load(2, enc_h, enc), load(3, ctx_h, ctx)
    load_og.start()

    @pl.loop(0, K)
    def _(i):
        o = lax.rem(i + 1, K)
        load_dec(2 * chip(o) + 1 - c).start()
        load_dec(2 * chip(o) + c).start()

    barrier = pltpu.get_barrier_semaphore()
    MESH = pl.DeviceIdType.MESH
    pl.semaphore_signal(barrier, inc=1, device_id={"tensor": mate}, device_id_type=MESH)

    @pl.loop(1, K)
    def _(o):
        pl.semaphore_signal(barrier, inc=1, device_id={"tensor": 2 * chip(o) + c}, device_id_type=MESH)

    @pl.loop(1, R)
    def _(o):
        pl.semaphore_signal(barrier, inc=1, device_id={"dp": lax.rem(d + o, R)}, device_id_type=MESH)

    pl.semaphore_wait(barrier, 1 + (K - 1) + (R - 1))

    def pair_copy(o, ch):
        return remote(pair_out.at[o, ch], pair_in.at[o, ch],
                      pair_ss.at[o, ch], pair_rs.at[o, ch], tensor=mate)

    def chip_copy(o, ch):
        return remote(chip_out.at[o, ch], chip_in.at[o, ch],
                      chip_ss.at[o, ch], chip_rs.at[o, ch], tensor=2 * chip(o) + c)

    load_w.start()
    load_enc.start()
    load_ctx.start()
    load_og.wait()

    def for_mate(o):
        j = 2 * chip(o) + 1 - c
        load_dec(j).wait()

        @pl.loop(0, CHUNKS)
        def _(ch):
            pair_out[o, ch] = dot(og[...], dec[codes_of(j, ch), :], 1, 1).astype(BF16)
            pair_copy(o, ch).start()

    @pl.loop(1, K)
    def _(o):
        for_mate(o)
        j = 2 * chip(o) + c
        load_dec(j).wait()

        @pl.loop(0, CHUNKS)
        def _(ch):
            cg_own[ch] = dot(og[...], dec[codes_of(j, ch), :], 1, 1)
            pair_copy(o, ch).wait_recv()
            chip_out[o, ch] = (cg_own[ch] + pair_in[o, ch].astype(F32)).astype(BF16)
            chip_copy(o, ch).start()

    for_mate(0)
    load_dec(t).wait()

    @pl.loop(0, CHUNKS)
    def _(ch):
        cg_own[ch] = dot(og[...], dec[codes_of(t, ch), :], 1, 1)

    load_w.wait()
    load_enc.wait()
    we[...] = dot(w[...], enc[...], 1, 0).astype(BF16)
    load_ctx.wait()

    def near_copy(j):
        return remote(codes.at[j], codes.at[j], near_ss, code_rs.at[j, 0], tensor=mate)

    def far_copy(j, o, ch):
        return remote(codes.at[j, rows(ch), :], codes.at[j, rows(ch), :],
                      far_ss.at[o, ch], code_rs.at[j, ch], tensor=2 * chip(o) + c)

    def fwd_copy(j, o, ch):
        return remote(codes.at[j, rows(ch), :], codes.at[j, rows(ch), :],
                      fwd_ss.at[o, ch], code_rs.at[j, ch], tensor=mate)

    codes[t] = dot(ctx[...], we[...], 1, 0).astype(BF16)
    near_copy(t).start()

    def sum_copy(o, ch):
        return remote(gt_out.at[ch, piece(lax.rem(d + o, R)), :], gt_in.at[ch, o],
                      sum_ss.at[o, ch], sum_rs.at[o, ch], dp=lax.rem(d + o, R))

    def all_copy(r, o, ch):
        return remote(gt_all.at[ch, piece(r), :], gt_all.at[ch, piece(r), :],
                      all_ss.at[o, ch], all_rs.at[o, ch], dp=lax.rem(d + o, R))

    for ch in range(CHUNKS):
        pair_copy(0, ch).wait_recv()
        cg_own[ch] += pair_in[0, ch].astype(F32)

        @pl.loop(1, K)
        def _(o):
            chip_copy(o, ch).wait_recv()
            cg_own[ch] += chip_in[o, ch].astype(F32)

        if ch == CHUNKS - 1:
            @pl.loop(1, K)
            def _(o):
                @pl.loop(0, CHUNKS)
                def _(part_of):
                    chip_copy(o, part_of).wait_send()
                    far_copy(t, o, part_of).start()

        cg[ch] = cg_own[ch].astype(BF16)
        gt_own[ch] = dot(ctx[...], cg[ch], 0, 0)
        gt_out[ch] = gt_own[ch].astype(BF16)

        @pl.loop(1, R)
        def _(o):
            sum_copy(o, ch).start()

    def total(ch):
        @pl.loop(1, R)
        def _(o):
            sum_copy(o, ch).wait_recv()
            gt_own[ch, piece(d), :] += gt_in[ch, o].astype(F32)

        gt_all[ch, piece(d), :] = gt_own[ch, piece(d), :].astype(BF16)

        @pl.loop(1, R)
        def _(o):
            all_copy(d, o, ch).start()

    @pl.loop(0, CHUNKS)
    def _(ch):
        acc[rows(ch), :] = dot(codes[t, rows(ch), :], dec[block(t), :], 1, 0)

    near_copy(mate).wait_recv()

    @pl.loop(0, CHUNKS)
    def _(ch):
        acc[rows(ch), :] += dot(codes[mate, rows(ch), :], dec[block(mate), :], 1, 0)

    total(0)
    gctx[...] = sum(
        dot(cg[ch], we[:, ch * cut:(ch + 1) * cut], 1, 1) for ch in range(CHUNKS)
    ).astype(BF16)
    store_gctx = pltpu.make_async_copy(gctx, gctx_h, store_sem.at[0])
    store_gctx.start()
    for ch in range(1, CHUNKS):
        total(ch)

    @pl.loop(0, CHUNKS)
    def _(ch):
        @pl.loop(1, K)
        def _(o):
            j = 2 * lax.rem(k - o + K, K) + c
            far_copy(j, o, ch).wait_recv()
            fwd_copy(j, o, ch).start()
            acc[rows(ch), :] += dot(codes[j, rows(ch), :], dec[block(j), :], 1, 0)

    mine = pl.ds(pl.multiple_of(d * own_rows, own_rows), own_rows)
    for ch in range(CHUNKS):
        @pl.loop(1, R)
        def _(o):
            all_copy(lax.rem(d - o + R, R), o, ch).wait_recv()

        term = dot(enc[mine, ch * cut:(ch + 1) * cut], gt_all[ch], 1, 1) * (1.0 / R)
        gw[...] = term if ch == 0 else gw[...] + term

    store_gw = pltpu.make_async_copy(gw, gw_h, store_sem.at[1])
    store_gw.start()

    def store_mixed(ch):
        return pltpu.make_async_copy(mixed.at[rows(ch), :], mixed_h.at[rows(ch), :], mix_sem.at[ch])

    @pl.loop(0, CHUNKS)
    def _(ch):
        @pl.loop(1, K)
        def _(o):
            j = 2 * lax.rem(k - o + K, K) + 1 - c
            fwd_copy(j, o, ch).wait_recv()
            acc[rows(ch), :] += dot(codes[j, rows(ch), :], dec[block(j), :], 1, 0)

        mixed[rows(ch), :] = acc[rows(ch), :].astype(BF16)
        store_mixed(ch).start()

    near_copy(t).wait_send()

    @pl.loop(0, CHUNKS)
    def _(ch):
        pair_copy(0, ch).wait_send()

        @pl.loop(1, K)
        def _(o):
            pair_copy(o, ch).wait_send()
            far_copy(t, o, ch).wait_send()
            fwd_copy(2 * lax.rem(k - o + K, K) + c, o, ch).wait_send()

        store_mixed(ch).wait()

    @pl.loop(1, R)
    def _(o):
        for ch in range(CHUNKS):
            sum_copy(o, ch).wait_send()
            all_copy(d, o, ch).wait_send()

    store_gctx.wait()
    store_gw.wait()


def hand_over(a, b, c, x, y, z):
    x[...], y[...], z[...] = a[...], b[...], c[...]


def on_device(S, R, context, w_out, encoder, decoder, out_grad):
    T, HW = context.shape
    D, C = encoder.shape
    DL = out_grad.shape[1]
    K, N = S // 2, CHUNKS
    hbm = pl.BlockSpec(memory_space=pl.ANY)
    dma = pltpu.SemaphoreType.DMA
    shapes = [
        ((T, HW), BF16), ((HW, D), BF16), ((D, C), BF16), ((S * C, DL), BF16), ((T, DL), BF16),
        ((HW, C), BF16), ((S, T, C), BF16),
        ((K, N, T, C // N), BF16), ((K, N, T, C // N), BF16),
        ((K, N, T, C // N), BF16), ((K, N, T, C // N), BF16),
        ((N, T, C // N), F32), ((N, T, C // N), BF16),
        ((N, HW, C // N), F32), ((N, HW, C // N), BF16),
        ((N, R, HW // R, C // N), BF16), ((N, HW, C // N), BF16),
        ((T, DL), F32), ((T, DL), BF16), ((T, HW), BF16), ((D // R, HW), F32),
    ]
    sems = [
        dma((4,)), dma((S,)), dma((2,)), dma((CHUNKS,)),
        dma((K, CHUNKS)), dma((K, CHUNKS)), dma((K, CHUNKS)), dma((K, CHUNKS)),
        dma, dma((K, CHUNKS)), dma((K, CHUNKS)), dma((S, CHUNKS)),
        dma((R, N)), dma((R, N)), dma((R, N)), dma((R, N)),
    ]
    out_shape = (
        jax.ShapeDtypeStruct((T, DL), BF16),
        jax.ShapeDtypeStruct((T, HW), BF16),
        jax.ShapeDtypeStruct((D // R, HW), F32),
    )
    results = pl.pallas_call(
        functools.partial(kernel, S, R),
        out_shape=out_shape,
        in_specs=[hbm] * 5,
        out_specs=(hbm,) * 3,
        scratch_shapes=[pltpu.VMEM(s, dt) for s, dt in shapes] + sems,
        compiler_params=pltpu.CompilerParams(
            collective_id=0, has_side_effects=True, vmem_limit_bytes=56 * 1024 * 1024
        ),
        cost_estimate=pl.CostEstimate(flops=6_000_000_000, bytes_accessed=14_000_000, transcendentals=0),
    )(context, w_out, encoder, decoder, out_grad)
    return pl.pallas_call(
        hand_over,
        out_shape=out_shape,
        grid=(PARTS,),
        in_specs=[pl.BlockSpec((s.shape[0] // PARTS, s.shape[1]), lambda i: (i, 0)) for s in out_shape],
        out_specs=tuple(pl.BlockSpec((s.shape[0] // PARTS, s.shape[1]), lambda i: (i, 0)) for s in out_shape),
        cost_estimate=pl.CostEstimate(flops=0, bytes_accessed=4_000_000, transcendentals=0),
    )(*results)


def solution(mesh):
    S, R = mesh.shape["tensor"], mesh.shape["dp"]
    in_specs = (P("dp", "tensor"), P("tensor", None), P(), P(None, "tensor"), P("dp", "tensor"))
    out_specs = (P("dp", "tensor"), P("dp", "tensor"), P("dp", "tensor"))
    return jax.shard_map(
        functools.partial(on_device, S, R), mesh=mesh, in_specs=in_specs, out_specs=out_specs, check_vma=False
    )
```
